512 devices in a mesh: blk: 16 (over x, y_hi, core), shard: 32 (over y_lo, z).
Axes of the slice: x: 4, y: 4 (y_hi: 2, y_lo: 2; y = y_hi * 2 + y_lo), z: 16, core: 2. Of those that a mesh axis runs over, the one named last changes fastest.
Arguments:
- hidden: bfloat16 [1024, 16384], P('shard', 'blk'), may hold values from -60 to 60
- proj_weight: bfloat16 [1024, 128], P('shard'), may hold values from -0.1875 to 0.1875
- passages: bfloat16 [4096, 128, 128], P(('blk', 'shard')), may hold values from -2.5 to 2.5
- cands: int32 [16, 32, 512, 4], P('blk', 'shard'), may hold values from 0 to 7, as said below
- counts: int32 [16, 32, 512], P('blk', 'shard'), may hold values from 0 to 4, as said below
- permitted: int32 [16, 512], P('blk'), may hold values 0 or 1
Outputs:
- best_scores: float32 [512, 128], P(('blk', 'shard'))
The draws below stay inside these ranges and needn't reach their ends.
Inputs may be any that keep to these rules, and one draw needn't show every extreme that they name: `cands`: the 4 slots of one list name distinct passages of one device's 8. `counts`: slots at or after a list's count are padding.
All inputs are finite; a program needn't handle non-finite values. No bound on the sum of `permitted` on one device may be relied on, other than what follows from the above.
Results may differ from the reference program's by a relative error of at most 0.0003.
Values may be sent and summed in bfloat16 or wider, within the bound.
No kernel may reach another device: no remote copies, remote signals or barrier semaphores. Data moves between devices by JAX's collectives and lax.ppermute only.
A program may use at most 64 MiB of HBM per device.

```python
import math
import jax
import jax.numpy as jnp
from jax import lax

DIM = 128
HID = 1024
QT = 32
PT = 128
CAND = 4
K = 128
P_DEV = 8
GROUPS = 16
LANES = 32
QUERIES = 512
PASSAGES = 4096


def draw_hidden(key, part):
    key = jax.random.fold_in(key, 101)
    first, second = jax.random.split(key, 2)
    scales = jnp.exp(jax.random.uniform(second, (1, QUERIES * QT), jnp.float32, 0.0, math.log(10.0)))
    values = jax.random.truncated_normal(first, -6.0, 6.0, (HID, QUERIES * QT), jnp.float32) * scales
    return values.astype(jnp.bfloat16)


def draw_passages(key, part):
    key = jax.random.fold_in(key, 202)
    first, second, third = jax.random.split(key, 3)
    low, high = (math.log(0.5), math.log(2.0))
    base = jax.random.truncated_normal(first, -4.0, 4.0, (PASSAGES, PT, DIM), jnp.float32)
    passage_scale = jnp.exp(jax.random.uniform(second, (PASSAGES, 1, 1), jnp.float32, low, high))
    token_scale = jnp.exp(jax.random.uniform(third, (PASSAGES, PT, 1), jnp.float32, math.log(0.5), math.log(2.0)))
    return (base * passage_scale * token_scale / math.sqrt(DIM)).astype(jnp.bfloat16)


def draw_cands(key, part):
    key = jax.random.fold_in(key, 303)
    noise = jax.random.randint(key, (GROUPS, LANES, QUERIES, P_DEV), 0, 1 << 20)
    keyed = noise * P_DEV + jnp.arange(P_DEV, dtype=jnp.int32)
    order = jnp.argsort(keyed, axis=-1, stable=True)
    return order[..., :CAND].astype(jnp.int32)


def draw_counts(key, part):
    key = jax.random.fold_in(key, 404)
    first, second, third = jax.random.split(key, 3)
    device_cap = jax.random.randint(first, (GROUPS, LANES, 1), 2, CAND + 1)
    fraction = jax.random.randint(second, (GROUPS, LANES, QUERIES), 1, CAND + 1)
    values = fraction * device_cap // CAND
    place = jax.random.randint(third, (3,), 0, 1 << 20)
    group_pick = place[0] % GROUPS
    lane_pick = place[1] % LANES
    query_pick = place[2] % QUERIES
    group_grid = jnp.arange(GROUPS, dtype=jnp.int32)[:, None, None]
    lane_grid = jnp.arange(LANES, dtype=jnp.int32)[None, :, None]
    query_grid = jnp.arange(QUERIES, dtype=jnp.int32)[None, None, :]
    chosen = (group_grid == group_pick) & (lane_grid == lane_pick) & (query_grid == query_pick)
    return jnp.where(chosen, CAND, values).astype(jnp.int32)


def set_ends(array, own_key, least, largest):
    spot = [jax.random.randint(jax.random.fold_in(own_key, axis), (), 0, length) for axis, length in enumerate(array.shape)]
    widest = array.shape.index(max(array.shape))
    neighbour = spot[:widest] + [(spot[widest] + 1) % array.shape[widest]] + spot[widest + 1:]
    return array.at[tuple(spot)].set(least).at[tuple(neighbour)].set(largest)


def level_of(key, extent, cuts, smallest, top_value):
    gain, own = 1.0, jax.random.fold_in(key, 6)
    for dim, shards_of in cuts:
        draws = jnp.exp(jax.random.uniform(jax.random.fold_in(own, dim), (shards_of,), jnp.float32, smallest / len(cuts), top_value / len(cuts)))
        gain = gain * jnp.repeat(draws, extent[dim] // shards_of).reshape([-1 if axis == dim else 1 for axis in range(len(extent))])
    return gain


def gaussian(own_key, shape, spread, bound, pieces=(), held_as=jnp.bfloat16):
    values = jax.random.normal(own_key, shape, jnp.float32) * spread
    if len(pieces) > 0:
        values = level_of(own_key, shape, pieces, -0.22, 0.18) * values
    return jnp.clip(values, min=-bound, max=bound).astype(held_as)


def setup_inputs(seed: int = 0) -> dict:
    seeds = jax.random.split(jax.random.key(seed), 7)
    return {
        "hidden": draw_hidden(jax.random.fold_in(seeds[6], 71), 0),
        "proj_weight": gaussian(seeds[1], (HID, DIM), HID ** -0.5, 0.1875, ((0, 32),)),
        "passages": draw_passages(jax.random.fold_in(seeds[6], 71), 0),
        "cands": draw_cands(jax.random.fold_in(seeds[6], 71), 0),
        "counts": draw_counts(jax.random.fold_in(seeds[6], 71), 0),
        "permitted": set_ends((jax.random.randint(seeds[5], (GROUPS, QUERIES), 0, 4) < 3).astype(jnp.int32), jax.random.fold_in(seeds[5], 1), 0, 1),
    }


def normalize(projected):
    squares_sum = lax.optimization_barrier(jnp.sum(projected * projected, axis=1, keepdims=True))
    return (projected * lax.rsqrt(squares_sum + 1e-06)).astype(jnp.bfloat16)

def reference(hidden, proj_weight, passages, cands, counts, permitted):
    projected = jnp.dot(hidden.T, proj_weight, preferred_element_type=jnp.float32)
    query_rows = normalize(projected)
    stock_table = passages.reshape(GROUPS * LANES, P_DEV * PT, DIM)
    slot_table = cands.reshape(GROUPS * LANES, QUERIES, CAND)

    def device_scores(inputs):
        passage_rows, slot_lists = inputs
        similarity = jnp.dot(query_rows, passage_rows.T, preferred_element_type=jnp.float32)
        best_table = lax.optimization_barrier(jnp.sum(lax.optimization_barrier(jnp.max(similarity.reshape(QUERIES, QT, P_DEV, PT), axis=3)), axis=1))
        return jnp.take_along_axis(best_table, slot_lists.astype(jnp.int32), axis=1)
    scores = lax.map(device_scores, (stock_table, slot_table)).reshape(GROUPS, LANES, QUERIES, CAND)
    slot_index = jnp.arange(CAND, dtype=jnp.int32)
    live_mask = (slot_index[None, None, None, :] < counts[:, :, :, None]) & (permitted[:, None, :, None] == 1)
    entries = jnp.where(live_mask, scores, jnp.zeros_like(scores))
    per_query = jnp.transpose(entries, (2, 0, 1, 3)).reshape(QUERIES, GROUPS * LANES * CAND)
    padded = jnp.concatenate([per_query, jnp.zeros((QUERIES, K), per_query.dtype)], axis=1)
    return lax.top_k(padded, K)[0]
```

```python
import jax
import jax.numpy as jnp
from jax import lax
from jax.experimental import pallas as pl
from jax.experimental.pallas import tpu as pltpu
from jax.sharding import PartitionSpec as P

DIM = 128
HID = 1024
QT = 32
PT = 128
CAND = 4
K = 128
P_DEV = 8
GROUPS = 16
LANES = 32
QUERIES = 512
TOK = QUERIES // GROUPS * QT
HID_DEV = HID // LANES
STOCK_ROWS = P_DEV * PT
MASK_ROWS = P_DEV * QUERIES // 128
ROWS = STOCK_ROWS + MASK_ROWS
HALF = GROUPS // 2
FOLD = 128 // QT
FOLD_ROWS = HID_DEV // FOLD


def vmem():
    return pl.BlockSpec(memory_space=pltpu.VMEM)


def lane_index(shape):
    return lax.broadcasted_iota(jnp.int32, shape, 1)


def row_index(shape):
    return lax.broadcasted_iota(jnp.int32, shape, 0)


def stock_kernel(passages, cands, counts, permitted, out):
    out[0:STOCK_ROWS, :] = passages[...]
    slots = row_index((P_DEV, QUERIES))
    allowed = permitted[...] == 1
    counted = counts[...]
    live = jnp.zeros((P_DEV, QUERIES), jnp.float32)
    for j in range(CAND):
        use = jnp.where(allowed & (counted > j), cands[j : j + 1, :], -1)
        live = jnp.where(use == slots, 1.0, live)
    parts = [live[:, 128 * b : 128 * (b + 1)] for b in range(QUERIES // 128)]
    out[STOCK_ROWS:ROWS, :] = jnp.concatenate(parts, axis=0).astype(jnp.bfloat16)


def stock(passages, cands, counts, permitted):
    return pl.pallas_call(
        stock_kernel,
        out_shape=jax.ShapeDtypeStruct((ROWS, DIM), jnp.bfloat16),
        in_specs=[vmem()] * 4,
        out_specs=vmem(),
        name="stock",
    )(passages, cands, counts, permitted)


def pack_kernel(hidden, weight, out):
    weight_rows = weight[...].astype(jnp.float32)
    slot = lane_index((FOLD_ROWS, 128)) // QT
    for tile in range(TOK // 128):
        block = hidden[:, 128 * tile : 128 * (tile + 1)].astype(jnp.float32)
        bands = [block[FOLD_ROWS * c : FOLD_ROWS * (c + 1), :] for c in range(FOLD)]
        for k in range(FOLD):
            folded = bands[k]
            for c in range(FOLD):
                if c != k:
                    moved = pltpu.roll(bands[c], (QT * (c - k)) % 128, 1)
                    folded = jnp.where(slot == c, moved, folded)
            both = jnp.concatenate([folded, weight_rows], axis=0)
            out[tile * FOLD + k] = both.astype(jnp.bfloat16)


def pack(hidden, weight):
    return pl.pallas_call(
        pack_kernel,
        out_shape=jax.ShapeDtypeStruct((LANES, FOLD_ROWS + HID_DEV, 128), jnp.bfloat16),
        in_specs=[vmem()] * 2,
        out_specs=vmem(),
        name="pack",
    )(hidden, weight)


def project_kernel(packed, out):
    hidden_rows = []
    weight_rows = [[] for _ in range(FOLD)]
    for source in range(LANES):
        block = packed[source].astype(jnp.float32)
        hidden_rows.append(block[0:FOLD_ROWS])
        for c in range(FOLD):
            start = FOLD_ROWS * (1 + c)
            weight_rows[c].append(block[start : start + FOLD_ROWS])
    hidden = jnp.concatenate(hidden_rows, axis=0).astype(jnp.bfloat16)
    projected = jnp.zeros((QT, DIM), jnp.float32)
    for c in range(FOLD):
        weight = jnp.concatenate(weight_rows[c], axis=0).astype(jnp.bfloat16)
        product = lax.dot_general(
            hidden, weight, (((0,), (0,)), ((), ())), preferred_element_type=jnp.float32
        )
        projected = projected + product[QT * c : QT * (c + 1), :]
    squares = jnp.sum(projected * projected, axis=1, keepdims=True)
    rows = (projected * lax.rsqrt(squares + 1e-06)).astype(jnp.bfloat16)
    for lane in range(LANES):
        out[lane] = rows


def project(packed):
    return pl.pallas_call(
        project_kernel,
        out_shape=jax.ShapeDtypeStruct((LANES, QT, DIM), jnp.bfloat16),
        in_specs=[vmem()],
        out_specs=vmem(),
        name="project",
    )(packed)


def three_parts(value):
    first = value.astype(jnp.bfloat16)
    rest = value - first.astype(jnp.float32)
    second = rest.astype(jnp.bfloat16)
    third = (rest - second.astype(jnp.float32)).astype(jnp.bfloat16)
    return first, second, third


def score_kernel(group, queries, mine, theirs, out, turned, best, masks):
    step = pl.program_id(0)

    @pl.when(step == 0)
    def _():
        turned[...] = queries[...].astype(jnp.float32).T.astype(jnp.bfloat16)

    quarter = group[0] // FOLD
    for side, block in enumerate((mine, theirs)):
        for c in range(TOK // 256):
            part = turned[:, 256 * c : 256 * (c + 1)]
            similarity = jnp.dot(
                block[0:STOCK_ROWS, :], part, preferred_element_type=jnp.float32
            )
            top = jnp.max(similarity.reshape(P_DEV, PT, 256), axis=1)
            best[side, step, :, 256 * c : 256 * (c + 1)] = top
        mask = block[STOCK_ROWS:ROWS, :].astype(jnp.float32)
        picked = mask[0:P_DEV]
        for b in range(1, QUERIES // 128):
            picked = jnp.where(quarter == b, mask[P_DEV * b : P_DEV * (b + 1)], picked)
        masks[side, step] = picked

    @pl.when(step == HALF - 1)
    def _():
        tops = best[...].reshape(GROUPS * P_DEV, TOK)
        member = (row_index((QT, TOK)) == lane_index((QT, TOK)) // QT).astype(jnp.bfloat16)
        scores = jnp.zeros((QT, 128), jnp.float32)
        for part in three_parts(tops):
            scores = scores + lax.dot_general(
                member, part, (((1,), (1,)), ((), ())), preferred_element_type=jnp.float32
            )
        wanted = (group[0] % FOLD) * QT + row_index((QT, 128))
        chosen = (lane_index((QT, 128)) == wanted).astype(jnp.bfloat16)
        live = lax.dot_general(
            chosen,
            masks[...].reshape(128, 128).astype(jnp.bfloat16),
            (((1,), (1,)), ((), ())),
            preferred_element_type=jnp.float32,
        )
        out[...] = jnp.where(live > 0.5, scores, 0.0)


def score(group, queries, mine, theirs):
    return pl.pallas_call(
        score_kernel,
        out_shape=jax.ShapeDtypeStruct((QT, 128), jnp.float32),
        grid=(HALF,),
        in_specs=[
            pl.BlockSpec(memory_space=pltpu.SMEM),
            pl.BlockSpec((TOK, DIM), lambda i: (0, 0)),
            pl.BlockSpec((ROWS, DIM), lambda i: (i, 0)),
            pl.BlockSpec((ROWS, DIM), lambda i: (i, 0)),
        ],
        out_specs=pl.BlockSpec((QT, 128), lambda i: (0, 0)),
        scratch_shapes=[
            pltpu.VMEM((DIM, TOK), jnp.bfloat16),
            pltpu.VMEM((2, HALF, P_DEV, TOK), jnp.float32),
            pltpu.VMEM((2, HALF, P_DEV, 128), jnp.float32),
        ],
        name="score",
    )(group, queries, mine, theirs)


def split_exchange(arrays, distance):
    count = len(arrays)
    if distance < count:
        result = list(arrays)
        for i in range(count):
            if not i & distance:
                result[i] = jnp.maximum(arrays[i], arrays[i + distance])
                result[i + distance] = jnp.minimum(arrays[i], arrays[i + distance])
        return result
    rows = distance // count
    upper = (row_index((8, 128)) & rows) != 0
    result = []
    for array in arrays:
        down = pltpu.roll(array, rows, 0)
        partner = down if 2 * rows == 8 else jnp.where(upper, down, pltpu.roll(array, 8 - rows, 0))
        result.append(jnp.where(upper, jnp.minimum(array, partner), jnp.maximum(array, partner)))
    return result


def select_kernel(table, out):
    arrays = []
    for v in range(LANES // 8):
        base = table[8 * v : 8 * (v + 1), :]
        arrays.append(base)
        for k in range(1, FOLD):
            arrays.append(pltpu.roll(base, QT * k, 1))
    arrays = [jnp.maximum(array, 0.0) for array in arrays]
    count = len(arrays)
    rows = row_index((8, 128))
    lanes = lane_index((8, 128))

    def signs(bit):
        return jnp.where((lanes & bit) != 0, -1.0, 1.0)

    column_sign = signs(16)
    arrays = [array * column_sign for array in arrays]
    size = 2
    while size <= K:
        flips = []
        for i in range(count):
            if size < count:
                flips.append(-1.0 if i & size else 1.0)
            elif size < K:
                flips.append(jnp.where((rows & (size // count)) != 0, -1.0, 1.0))
            else:
                flips.append(1.0)

        def flipped(values):
            return [v if isinstance(f, float) and f == 1.0 else v * f for v, f in zip(values, flips)]

        arrays = flipped(arrays)
        distance = size // 2
        while distance:
            arrays = split_exchange(arrays, distance)
            distance //= 2
        arrays = flipped(arrays)
        size *= 2
    width = 16
    while width:
        arrays = [array * column_sign for array in arrays]
        arrays = [jnp.maximum(array, pltpu.roll(array, width, 1)) for array in arrays]
        width //= 2
        if width:
            column_sign = signs(width)
            arrays = [array * column_sign for array in arrays]
        distance = K // 2
        while distance:
            arrays = split_exchange(arrays, distance)
            distance //= 2
    total = jnp.zeros((8, 128), jnp.float32)
    for i, array in enumerate(arrays):
        total = total + jnp.where(lanes == rows * count + i, array, 0.0)
    out[...] = jnp.sum(total, axis=0, keepdims=True)


def select(table):
    return pl.pallas_call(
        select_kernel,
        out_shape=jax.ShapeDtypeStruct((1, K), jnp.float32),
        in_specs=[vmem()],
        out_specs=vmem(),
        name="select",
    )(table)


def body(hidden, proj_weight, passages, cands, counts, permitted):
    group = lax.axis_index("blk").astype(jnp.int32).reshape(1)
    slots = cands.reshape(QUERIES, CAND).T
    own = stock(
        passages.reshape(STOCK_ROWS, DIM), slots, counts.reshape(1, QUERIES), permitted
    )
    same_core = [list(range(core, GROUPS, 2)) for core in range(2)]
    mine = lax.all_gather(own, "blk", axis=0, tiled=True, axis_index_groups=same_core)
    packed = lax.all_to_all(pack(hidden, proj_weight), "shard", 0, 0, tiled=True)
    rows = project(packed)
    theirs = lax.ppermute(mine, "blk", [(i, i ^ 1) for i in range(GROUPS)])
    queries = lax.all_to_all(rows, "shard", 0, 0, tiled=True).reshape(TOK, DIM)
    table = score(group, queries, mine, theirs)
    entries = lax.all_to_all(table.reshape(LANES, 1, 128), "shard", 0, 0, tiled=True)
    return select(entries.reshape(LANES, 128))


def solution(mesh):
    in_specs = (
        P("shard", "blk"),
        P("shard", None),
        P(("blk", "shard"), None, None),
        P("blk", "shard", None, None),
        P("blk", "shard", None),
        P("blk", None),
    )
    out_specs = P(("blk", "shard"), None)
    return jax.shard_map(body, mesh=mesh, in_specs=in_specs, out_specs=out_specs, check_vma=False)
```

```python
import jax
import jax.numpy as jnp
from jax import lax
from jax.experimental import pallas as pl
from jax.experimental.pallas import tpu as pltpu
from jax.sharding import PartitionSpec as P

DIM = 128
HID = 1024
QT = 32
PT = 128
CAND = 4
K = 128
P_DEV = 8
GROUPS = 16
LANES = 32
QUERIES = 512
TOK = QUERIES // GROUPS * QT
HID_DEV = HID // LANES
STOCK_ROWS = P_DEV * PT
MASK_ROWS = P_DEV * QUERIES // 128
ROWS = STOCK_ROWS + MASK_ROWS
HALF = GROUPS // 2
STEPS = GROUPS // 4
FOLD = 128 // QT
FOLD_ROWS = HID_DEV // FOLD


def vmem():
    return pl.BlockSpec(memory_space=pltpu.VMEM)


def lane_index(shape):
    return lax.broadcasted_iota(jnp.int32, shape, 1)


def row_index(shape):
    return lax.broadcasted_iota(jnp.int32, shape, 0)


def stock_kernel(passages, cands, counts, permitted, out):
    out[0:STOCK_ROWS, :] = passages[...]
    slots = row_index((P_DEV, QUERIES))
    allowed = permitted[...] == 1
    counted = counts[...]
    live = jnp.zeros((P_DEV, QUERIES), jnp.float32)
    for j in range(CAND):
        use = jnp.where(allowed & (counted > j), cands[j : j + 1, :], -1)
        live = jnp.where(use == slots, 1.0, live)
    parts = [live[:, 128 * b : 128 * (b + 1)] for b in range(QUERIES // 128)]
    out[STOCK_ROWS:ROWS, :] = jnp.concatenate(parts, axis=0).astype(jnp.bfloat16)


def stock(passages, cands, counts, permitted):
    return pl.pallas_call(
        stock_kernel,
        out_shape=jax.ShapeDtypeStruct((ROWS, DIM), jnp.bfloat16),
        in_specs=[vmem()] * 4,
        out_specs=vmem(),
        cost_estimate=pl.CostEstimate(
            flops=10**9, bytes_accessed=2 * ROWS * DIM * 2, transcendentals=0
        ),
        name="stock",
    )(passages, cands, counts, permitted)


def pack_kernel(hidden, weight, out):
    weight_rows = weight[...].astype(jnp.float32)
    slot = lane_index((FOLD_ROWS, 128)) // QT
    for tile in range(TOK // 128):
        block = hidden[:, 128 * tile : 128 * (tile + 1)].astype(jnp.float32)
        bands = [block[FOLD_ROWS * c : FOLD_ROWS * (c + 1), :] for c in range(FOLD)]
        for k in range(FOLD):
            folded = bands[k]
            for c in range(FOLD):
                if c != k:
                    moved = pltpu.roll(bands[c], (QT * (c - k)) % 128, 1)
                    folded = jnp.where(slot == c, moved, folded)
            both = jnp.concatenate([folded, weight_rows], axis=0)
            out[tile * FOLD + k] = both.astype(jnp.bfloat16)


def pack(hidden, weight):
    return pl.pallas_call(
        pack_kernel,
        out_shape=jax.ShapeDtypeStruct((LANES, FOLD_ROWS + HID_DEV, 128), jnp.bfloat16),
        in_specs=[vmem()] * 2,
        out_specs=vmem(),
        name="pack",
    )(hidden, weight)


def project_kernel(packed, out):
    hidden_rows = []
    weight_rows = [[] for _ in range(FOLD)]
    for source in range(LANES):
        block = packed[source].astype(jnp.float32)
        hidden_rows.append(block[0:FOLD_ROWS])
        for c in range(FOLD):
            start = FOLD_ROWS * (1 + c)
            weight_rows[c].append(block[start : start + FOLD_ROWS])
    hidden = jnp.concatenate(hidden_rows, axis=0).astype(jnp.bfloat16)
    projected = jnp.zeros((QT, DIM), jnp.float32)
    for c in range(FOLD):
        weight = jnp.concatenate(weight_rows[c], axis=0).astype(jnp.bfloat16)
        product = lax.dot_general(
            hidden, weight, (((0,), (0,)), ((), ())), preferred_element_type=jnp.float32
        )
        projected = projected + product[QT * c : QT * (c + 1), :]
    squares = jnp.sum(projected * projected, axis=1, keepdims=True)
    rows = (projected * lax.rsqrt(squares + 1e-06)).astype(jnp.bfloat16)
    for lane in range(LANES):
        out[lane] = rows


def project(packed):
    return pl.pallas_call(
        project_kernel,
        out_shape=jax.ShapeDtypeStruct((LANES, QT, DIM), jnp.bfloat16),
        in_specs=[vmem()],
        out_specs=vmem(),
        cost_estimate=pl.CostEstimate(
            flops=20 * 10**9, bytes_accessed=LANES * QT * DIM * 2, transcendentals=0
        ),
        name="project",
    )(packed)


def three_parts(value):
    first = value.astype(jnp.bfloat16)
    rest = value - first.astype(jnp.float32)
    second = rest.astype(jnp.bfloat16)
    third = (rest - second.astype(jnp.float32)).astype(jnp.bfloat16)
    return first, second, third


def score_kernel(group, queries, mine, theirs, out, turned, best, masks):
    step = pl.program_id(0)

    @pl.when(step == 0)
    def _():
        turned[...] = queries[...].astype(jnp.float32).T.astype(jnp.bfloat16)

    quarter = group[0] // FOLD
    for side, block in enumerate((mine, theirs)):
        for c in range(TOK // 256):
            part = turned[:, 256 * c : 256 * (c + 1)]
            similarity = jnp.dot(
                block[0:STOCK_ROWS, :], part, preferred_element_type=jnp.float32
            )
            top = jnp.max(similarity.reshape(P_DEV, PT, 256), axis=1)
            best[side, step, :, 256 * c : 256 * (c + 1)] = top
        mask = block[STOCK_ROWS:ROWS, :].astype(jnp.float32)
        picked = mask[0:P_DEV]
        for b in range(1, QUERIES // 128):
            picked = jnp.where(quarter == b, mask[P_DEV * b : P_DEV * (b + 1)], picked)
        masks[side, step] = picked

    @pl.when(step == STEPS - 1)
    def _():
        tops = best[...].reshape(HALF * P_DEV, TOK)
        member = (row_index((QT, TOK)) == lane_index((QT, TOK)) // QT).astype(jnp.bfloat16)
        scores = jnp.zeros((QT, HALF * P_DEV), jnp.float32)
        for part in three_parts(tops):
            scores = scores + lax.dot_general(
                member, part, (((1,), (1,)), ((), ())), preferred_element_type=jnp.float32
            )
        wanted = (group[0] % FOLD) * QT + row_index((QT, 128))
        chosen = (lane_index((QT, 128)) == wanted).astype(jnp.bfloat16)
        live = lax.dot_general(
            chosen,
            masks[...].reshape(HALF * P_DEV, 128).astype(jnp.bfloat16),
            (((1,), (1,)), ((), ())),
            preferred_element_type=jnp.float32,
        )
        out[...] = jnp.where(live > 0.5, scores, 0.0)


def score(group, queries, mine, theirs):
    return pl.pallas_call(
        score_kernel,
        out_shape=jax.ShapeDtypeStruct((QT, HALF * P_DEV), jnp.float32),
        grid=(STEPS,),
        in_specs=[
            pl.BlockSpec(memory_space=pltpu.SMEM),
            pl.BlockSpec((TOK, DIM), lambda i: (0, 0)),
            pl.BlockSpec((ROWS, DIM), lambda i: (i, 0)),
            pl.BlockSpec((ROWS, DIM), lambda i: (i, 0)),
        ],
        out_specs=pl.BlockSpec((QT, HALF * P_DEV), lambda i: (0, 0)),
        scratch_shapes=[
            pltpu.VMEM((DIM, TOK), jnp.bfloat16),
            pltpu.VMEM((2, STEPS, P_DEV, TOK), jnp.float32),
            pltpu.VMEM((2, STEPS, P_DEV, 128), jnp.float32),
        ],
        cost_estimate=pl.CostEstimate(
            flops=40 * 10**9, bytes_accessed=2 * STEPS * ROWS * DIM * 2, transcendentals=0
        ),
        name="score",
    )(group, queries, mine, theirs)


def split_exchange(arrays, distance):
    count = len(arrays)
    if distance < count:
        result = list(arrays)
        for i in range(count):
            if not i & distance:
                result[i] = jnp.maximum(arrays[i], arrays[i + distance])
                result[i + distance] = jnp.minimum(arrays[i], arrays[i + distance])
        return result
    rows = distance // count
    upper = (row_index((8, 128)) & rows) != 0
    result = []
    for array in arrays:
        down = pltpu.roll(array, rows, 0)
        partner = down if 2 * rows == 8 else jnp.where(upper, down, pltpu.roll(array, 8 - rows, 0))
        result.append(jnp.where(upper, jnp.minimum(array, partner), jnp.maximum(array, partner)))
    return result


def select_kernel(table, out):
    arrays = []
    for v in range(LANES // 8):
        base = table[8 * v : 8 * (v + 1), :]
        arrays.append(base)
        for k in range(1, FOLD):
            arrays.append(pltpu.roll(base, QT * k, 1))
    arrays = [jnp.maximum(array, 0.0) for array in arrays]
    count = len(arrays)
    rows = row_index((8, 128))
    lanes = lane_index((8, 128))

    def signs(bit):
        return jnp.where((lanes & bit) != 0, -1.0, 1.0)

    column_sign = signs(16)
    arrays = [array * column_sign for array in arrays]
    size = 2
    while size <= K:
        flips = []
        for i in range(count):
            if size < count:
                flips.append(-1.0 if i & size else 1.0)
            elif size < K:
                flips.append(jnp.where((rows & (size // count)) != 0, -1.0, 1.0))
            else:
                flips.append(1.0)

        def flipped(values):
            return [v if isinstance(f, float) and f == 1.0 else v * f for v, f in zip(values, flips)]

        arrays = flipped(arrays)
        distance = size // 2
        while distance:
            arrays = split_exchange(arrays, distance)
            distance //= 2
        arrays = flipped(arrays)
        size *= 2
    width = 16
    while width:
        arrays = [array * column_sign for array in arrays]
        arrays = [jnp.maximum(array, pltpu.roll(array, width, 1)) for array in arrays]
        width //= 2
        if width:
            column_sign = signs(width)
            arrays = [array * column_sign for array in arrays]
        distance = K // 2
        while distance:
            arrays = split_exchange(arrays, distance)
            distance //= 2
    total = jnp.zeros((8, 128), jnp.float32)
    for i, array in enumerate(arrays):
        total = total + jnp.where(lanes == rows * count + i, array, 0.0)
    out[...] = jnp.sum(total, axis=0, keepdims=True)


def select(table):
    return pl.pallas_call(
        select_kernel,
        out_shape=jax.ShapeDtypeStruct((1, K), jnp.float32),
        in_specs=[vmem()],
        out_specs=vmem(),
        name="select",
    )(table)


def turned(steps):
    return [(i, (i + steps) % GROUPS) for i in range(GROUPS)]


def body(hidden, proj_weight, passages, cands, counts, permitted):
    group = lax.axis_index("blk").astype(jnp.int32).reshape(1)
    slots = cands.reshape(QUERIES, CAND).T
    packed = pack(hidden, proj_weight)
    passages, packed = lax.optimization_barrier((passages, packed))
    own = stock(
        passages.reshape(STOCK_ROWS, DIM), slots, counts.reshape(1, QUERIES), permitted
    )
    along_x = [lax.ppermute(own, "blk", turned(4 * x)) for x in (1, 3, 2)]
    near = jnp.concatenate([own, *along_x])
    far = lax.ppermute(near, "blk", [(i, i ^ 2) for i in range(GROUPS)])
    other_core = [(i, i ^ 1) for i in range(GROUPS)]
    rows = project(lax.all_to_all(packed, "shard", 0, 0, tiled=True))
    held, rows = lax.optimization_barrier((near, rows))
    near_other = lax.ppermute(held, "blk", other_core)
    far_other = lax.ppermute(far, "blk", other_core)
    queries = lax.all_to_all(rows, "shard", 0, 0, tiled=True).reshape(TOK, DIM)
    first = score(group, queries, near, near_other)
    second = score(group, queries, far, far_other)
    table = jnp.concatenate([first, second], axis=1)
    entries = lax.all_to_all(table.reshape(LANES, 1, 128), "shard", 0, 0, tiled=True)
    return select(entries.reshape(LANES, 128))


def solution(mesh):
    in_specs = (
        P("shard", "blk"),
        P("shard", None),
        P(("blk", "shard"), None, None),
        P("blk", "shard", None, None),
        P("blk", "shard", None),
        P("blk", None),
    )
    out_specs = P(("blk", "shard"), None)
    return jax.shard_map(body, mesh=mesh, in_specs=in_specs, out_specs=out_specs, check_vma=False)
```

```python
import jax
import jax.numpy as jnp
from jax import lax
from jax.experimental import pallas as pl
from jax.experimental.pallas import tpu as pltpu
from jax.sharding import PartitionSpec as P

DIM = 128
HID = 1024
QT = 32
PT = 128
CAND = 4
K = 128
P_DEV = 8
GROUPS = 16
LANES = 32
QUERIES = 512
TOK = QUERIES // GROUPS * QT
HID_DEV = HID // LANES
STOCK_ROWS = P_DEV * PT
MASK_ROWS = P_DEV * QUERIES // 128
ROWS = STOCK_ROWS + MASK_ROWS
STEPS = GROUPS // 4
FOLD = 128 // QT
FOLD_ROWS = HID_DEV // FOLD


def vmem():
    return pl.BlockSpec(memory_space=pltpu.VMEM)


def limit(mebibytes):
    return pltpu.CompilerParams(vmem_limit_bytes=mebibytes * 2**20)


def lane_index(shape):
    return lax.broadcasted_iota(jnp.int32, shape, 1)


def row_index(shape):
    return lax.broadcasted_iota(jnp.int32, shape, 0)


def stock_kernel(passages, cands, counts, permitted, out):
    out[0:STOCK_ROWS, :] = passages[...]
    slots = row_index((P_DEV, QUERIES))
    allowed = permitted[...] == 1
    counted = counts[...]
    live = jnp.zeros((P_DEV, QUERIES), jnp.float32)
    for j in range(CAND):
        use = jnp.where(allowed & (counted > j), cands[j : j + 1, :], -1)
        live = jnp.where(use == slots, 1.0, live)
    parts = [live[:, 128 * b : 128 * (b + 1)] for b in range(QUERIES // 128)]
    out[STOCK_ROWS:ROWS, :] = jnp.concatenate(parts, axis=0).astype(jnp.bfloat16)


def pack_kernel(hidden, weight, out):
    weight_rows = weight[...].astype(jnp.float32)
    slot = lane_index((FOLD_ROWS, 128)) // QT
    for tile in range(TOK // 128):
        block = hidden[:, 128 * tile : 128 * (tile + 1)].astype(jnp.float32)
        bands = [block[FOLD_ROWS * c : FOLD_ROWS * (c + 1), :] for c in range(FOLD)]
        for k in range(FOLD):
            folded = bands[k]
            for c in range(FOLD):
                if c != k:
                    moved = pltpu.roll(bands[c], (QT * (c - k)) % 128, 1)
                    folded = jnp.where(slot == c, moved, folded)
            both = jnp.concatenate([folded, weight_rows], axis=0)
            out[tile * FOLD + k] = both.astype(jnp.bfloat16)


def prepare_kernel(hidden, weight, passages, cands, counts, permitted, packed, own):
    pack_kernel(hidden, weight, packed)
    stock_kernel(passages, cands, counts, permitted, own)


def prepare(hidden, weight, passages, cands, counts, permitted):
    return pl.pallas_call(
        prepare_kernel,
        out_shape=(
            jax.ShapeDtypeStruct((LANES, FOLD_ROWS + HID_DEV, 128), jnp.bfloat16),
            jax.ShapeDtypeStruct((ROWS, DIM), jnp.bfloat16),
        ),
        in_specs=[vmem()] * 6,
        out_specs=(vmem(), vmem()),
        compiler_params=limit(56),
        name="prepare",
    )(hidden, weight, passages, cands, counts, permitted)


def both_kernel(own, across, out):
    out[0:ROWS, :] = own[...]
    out[ROWS : 2 * ROWS, :] = across[...]


def both(own, across):
    return pl.pallas_call(
        both_kernel,
        out_shape=jax.ShapeDtypeStruct((2 * ROWS, DIM), jnp.bfloat16),
        in_specs=[vmem()] * 2,
        out_specs=vmem(),
        cost_estimate=pl.CostEstimate(
            flops=40 * 10**9, bytes_accessed=4 * ROWS * DIM * 2, transcendentals=0
        ),
        compiler_params=limit(8),
        name="both",
    )(own, across)


def all_four_kernel(*refs):
    for i, ref in enumerate(refs[:4]):
        refs[4][2 * ROWS * i : 2 * ROWS * (i + 1), :] = ref[...]


def all_four(*pairs):
    return pl.pallas_call(
        all_four_kernel,
        out_shape=jax.ShapeDtypeStruct((8 * ROWS, DIM), jnp.bfloat16),
        in_specs=[vmem()] * 4,
        out_specs=vmem(),
        cost_estimate=pl.CostEstimate(
            flops=10 * 10**9, bytes_accessed=16 * ROWS * DIM * 2, transcendentals=0
        ),
        compiler_params=limit(14),
        name="all_four",
    )(*pairs)


def project_kernel(packed, out):
    hidden_rows = []
    weight_rows = [[] for _ in range(FOLD)]
    for source in range(LANES):
        block = packed[source].astype(jnp.float32)
        hidden_rows.append(block[0:FOLD_ROWS])
        for c in range(FOLD):
            start = FOLD_ROWS * (1 + c)
            weight_rows[c].append(block[start : start + FOLD_ROWS])
    hidden = jnp.concatenate(hidden_rows, axis=0).astype(jnp.bfloat16)
    projected = jnp.zeros((QT, DIM), jnp.float32)
    for c in range(FOLD):
        weight = jnp.concatenate(weight_rows[c], axis=0).astype(jnp.bfloat16)
        product = lax.dot_general(
            hidden, weight, (((0,), (0,)), ((), ())), preferred_element_type=jnp.float32
        )
        projected = projected + product[QT * c : QT * (c + 1), :]
    squares = jnp.sum(projected * projected, axis=1, keepdims=True)
    rows = (projected * lax.rsqrt(squares + 1e-06)).astype(jnp.bfloat16)
    for lane in range(LANES):
        out[lane] = rows


def project(packed):
    return pl.pallas_call(
        project_kernel,
        out_shape=jax.ShapeDtypeStruct((LANES, QT, DIM), jnp.bfloat16),
        in_specs=[vmem()],
        out_specs=vmem(),
        cost_estimate=pl.CostEstimate(
            flops=20 * 10**9, bytes_accessed=LANES * QT * DIM * 2, transcendentals=0
        ),
        compiler_params=limit(8),
        name="project",
    )(packed)


def three_parts(value):
    first = value.astype(jnp.bfloat16)
    rest = value - first.astype(jnp.float32)
    second = rest.astype(jnp.bfloat16)
    third = (rest - second.astype(jnp.float32)).astype(jnp.bfloat16)
    return first, second, third


def turn_kernel(queries, out):
    out[...] = queries[...].astype(jnp.float32).T.astype(jnp.bfloat16)


def turn(queries):
    return pl.pallas_call(
        turn_kernel,
        out_shape=jax.ShapeDtypeStruct((DIM, TOK), jnp.bfloat16),
        in_specs=[vmem()],
        out_specs=vmem(),
        cost_estimate=pl.CostEstimate(
            flops=40 * 10**9, bytes_accessed=2 * TOK * DIM * 2, transcendentals=0
        ),
        compiler_params=limit(8),
        name="turn",
    )(queries)


def score_kernel(group, turned, *refs):
    blocks, (out, best, masks) = refs[:4], refs[4:]
    step = pl.program_id(0)

    quarter = group[0] // FOLD
    for side, block in enumerate(blocks):
        for c in range(TOK // 256):
            part = turned[:, 256 * c : 256 * (c + 1)]
            similarity = jnp.dot(
                block[0:STOCK_ROWS, :], part, preferred_element_type=jnp.float32
            )
            top = jnp.max(similarity.reshape(P_DEV, PT, 256), axis=1)
            best[side, step, :, 256 * c : 256 * (c + 1)] = top
        mask = block[STOCK_ROWS:ROWS, :].astype(jnp.float32)
        picked = mask[0:P_DEV]
        for b in range(1, QUERIES // 128):
            picked = jnp.where(quarter == b, mask[P_DEV * b : P_DEV * (b + 1)], picked)
        masks[side, step] = picked

    @pl.when(step == STEPS - 1)
    def _():
        tops = best[...].reshape(GROUPS * P_DEV, TOK)
        member = (row_index((QT, TOK)) == lane_index((QT, TOK)) // QT).astype(jnp.bfloat16)
        scores = jnp.zeros((QT, GROUPS * P_DEV), jnp.float32)
        for part in three_parts(tops):
            scores = scores + lax.dot_general(
                member, part, (((1,), (1,)), ((), ())), preferred_element_type=jnp.float32
            )
        wanted = (group[0] % FOLD) * QT + row_index((QT, 128))
        chosen = (lane_index((QT, 128)) == wanted).astype(jnp.bfloat16)
        live = lax.dot_general(
            chosen,
            masks[...].reshape(GROUPS * P_DEV, 128).astype(jnp.bfloat16),
            (((1,), (1,)), ((), ())),
            preferred_element_type=jnp.float32,
        )
        out[...] = jnp.where(live > 0.5, scores, 0.0)


def score(group, queries, mine, theirs):
    return pl.pallas_call(
        score_kernel,
        out_shape=jax.ShapeDtypeStruct((QT, GROUPS * P_DEV), jnp.float32),
        grid=(STEPS,),
        in_specs=[
            pl.BlockSpec(memory_space=pltpu.SMEM),
            pl.BlockSpec((DIM, TOK), lambda i: (0, 0)),
            *[pl.BlockSpec((ROWS, DIM), lambda i, at=at: (i + at, 0)) for at in (0, STEPS)] * 2,
        ],
        out_specs=pl.BlockSpec((QT, GROUPS * P_DEV), lambda i: (0, 0)),
        scratch_shapes=[
            pltpu.VMEM((4, STEPS, P_DEV, TOK), jnp.float32),
            pltpu.VMEM((4, STEPS, P_DEV, 128), jnp.float32),
        ],
        cost_estimate=pl.CostEstimate(
            flops=40 * 10**9, bytes_accessed=GROUPS * ROWS * DIM * 2, transcendentals=0
        ),
        compiler_params=limit(16),
        name="score",
    )(group, queries, mine, mine, theirs, theirs)


def split_exchange(arrays, distance):
    count = len(arrays)
    if distance < count:
        result = list(arrays)
        for i in range(count):
            if not i & distance:
                result[i] = jnp.maximum(arrays[i], arrays[i + distance])
                result[i + distance] = jnp.minimum(arrays[i], arrays[i + distance])
        return result
    rows = distance // count
    upper = (row_index((8, 128)) & rows) != 0
    result = []
    for array in arrays:
        down = pltpu.roll(array, rows, 0)
        partner = down if 2 * rows == 8 else jnp.where(upper, down, pltpu.roll(array, 8 - rows, 0))
        result.append(jnp.where(upper, jnp.minimum(array, partner), jnp.maximum(array, partner)))
    return result


def select_kernel(table, out):
    arrays = []
    for v in range(LANES // 8):
        base = table[8 * v : 8 * (v + 1), :]
        arrays.append(base)
        for k in range(1, FOLD):
            arrays.append(pltpu.roll(base, QT * k, 1))
    arrays = [jnp.maximum(array, 0.0) for array in arrays]
    count = len(arrays)
    rows = row_index((8, 128))
    lanes = lane_index((8, 128))

    def signs(bit):
        return jnp.where((lanes & bit) != 0, -1.0, 1.0)

    column_sign = signs(16)
    arrays = [array * column_sign for array in arrays]
    size = 2
    while size <= K:
        flips = []
        for i in range(count):
            if size < count:
                flips.append(-1.0 if i & size else 1.0)
            elif size < K:
                flips.append(jnp.where((rows & (size // count)) != 0, -1.0, 1.0))
            else:
                flips.append(1.0)

        def flipped(values):
            return [v if isinstance(f, float) and f == 1.0 else v * f for v, f in zip(values, flips)]

        arrays = flipped(arrays)
        distance = size // 2
        while distance:
            arrays = split_exchange(arrays, distance)
            distance //= 2
        arrays = flipped(arrays)
        size *= 2
    width = 16
    while width:
        arrays = [array * column_sign for array in arrays]
        arrays = [jnp.maximum(array, pltpu.roll(array, width, 1)) for array in arrays]
        width //= 2
        if width:
            column_sign = signs(width)
            arrays = [array * column_sign for array in arrays]
        distance = K // 2
        while distance:
            arrays = split_exchange(arrays, distance)
            distance //= 2
    total = jnp.zeros((8, 128), jnp.float32)
    for i, array in enumerate(arrays):
        total = total + jnp.where(lanes == rows * count + i, array, 0.0)
    out[...] = jnp.sum(total, axis=0, keepdims=True)


def select(table):
    return pl.pallas_call(
        select_kernel,
        out_shape=jax.ShapeDtypeStruct((1, K), jnp.float32),
        in_specs=[vmem()],
        out_specs=vmem(),
        compiler_params=limit(8),
        name="select",
    )(table)


def turned(steps):
    return [(i, (i + steps) % GROUPS) for i in range(GROUPS)]


def body(hidden, proj_weight, passages, cands, counts, permitted):
    group = lax.axis_index("blk").astype(jnp.int32).reshape(1)
    slots = cands.reshape(QUERIES, CAND).T
    packed, own = prepare(
        hidden,
        proj_weight,
        passages.reshape(STOCK_ROWS, DIM),
        slots,
        counts.reshape(1, QUERIES),
        permitted,
    )
    across = lax.ppermute(own, "blk", [(i, i ^ 2) for i in range(GROUPS)])
    pair = both(own, across)
    along_x = [lax.ppermute(pair, "blk", turned(4 * x)) for x in (1, 3, 2)]
    rows = project(lax.all_to_all(packed, "shard", 0, 0, tiled=True))
    mine = all_four(pair, *along_x)
    theirs = lax.ppermute(mine, "blk", [(i, i ^ 1) for i in range(GROUPS)])
    queries = lax.all_to_all(rows, "shard", 0, 0, tiled=True).reshape(TOK, DIM)
    table = score(group, turn(queries), mine, theirs)
    entries = lax.all_to_all(table.reshape(LANES, 1, 128), "shard", 0, 0, tiled=True)
    return select(entries.reshape(LANES, 128))


def solution(mesh):
    in_specs = (
        P("shard", "blk"),
        P("shard", None),
        P(("blk", "shard"), None, None),
        P("blk", "shard", None, None),
        P("blk", "shard", None),
        P("blk", None),
    )
    out_specs = P(("blk", "shard"), None)
    return jax.shard_map(body, mesh=mesh, in_specs=in_specs, out_specs=out_specs, check_vma=False)
```

```python
import jax
import jax.numpy as jnp
from jax import lax
from jax.experimental import pallas as pl
from jax.experimental.pallas import tpu as pltpu
from jax.sharding import PartitionSpec as P

DIM = 128
HID = 1024
QT = 32
PT = 128
CAND = 4
K = 128
P_DEV = 8
GROUPS = 16
LANES = 32
QUERIES = 512
TOK = QUERIES // GROUPS * QT
HID_DEV = HID // LANES
STOCK_ROWS = P_DEV * PT
MASK_ROWS = P_DEV * QUERIES // 128
ROWS = STOCK_ROWS + MASK_ROWS
STEPS = 2
SIDES = GROUPS // STEPS
FOLD = 128 // QT
FOLD_ROWS = HID_DEV // FOLD
FIRST = 8


def vmem():
    return pl.BlockSpec(memory_space=pltpu.VMEM)


def limit(mebibytes):
    return pltpu.CompilerParams(vmem_limit_bytes=mebibytes * 2**20)


def lane_index(shape):
    return lax.broadcasted_iota(jnp.int32, shape, 1)


def row_index(shape):
    return lax.broadcasted_iota(jnp.int32, shape, 0)


def stock_kernel(passages, cands, counts, permitted, out):
    out[0:STOCK_ROWS, :] = passages[...]
    slots = row_index((P_DEV, QUERIES))
    allowed = permitted[...] == 1
    counted = counts[...]
    live = jnp.zeros((P_DEV, QUERIES), jnp.float32)
    for j in range(CAND):
        use = jnp.where(allowed & (counted > j), cands[j : j + 1, :], -1)
        live = jnp.where(use == slots, 1.0, live)
    parts = [live[:, 128 * b : 128 * (b + 1)] for b in range(QUERIES // 128)]
    out[STOCK_ROWS:ROWS, :] = jnp.concatenate(parts, axis=0).astype(jnp.bfloat16)


def pack_kernel(hidden, weight, out):
    weight_rows = weight[...].astype(jnp.float32)
    slot = lane_index((FOLD_ROWS, 128)) // QT
    for tile in range(TOK // 128):
        block = hidden[:, 128 * tile : 128 * (tile + 1)].astype(jnp.float32)
        bands = [block[FOLD_ROWS * c : FOLD_ROWS * (c + 1), :] for c in range(FOLD)]
        for k in range(FOLD):
            folded = bands[k]
            for c in range(FOLD):
                if c != k:
                    moved = pltpu.roll(bands[c], (QT * (c - k)) % 128, 1)
                    folded = jnp.where(slot == c, moved, folded)
            both = jnp.concatenate([folded, weight_rows], axis=0)
            out[(tile * FOLD + k - FIRST) % LANES] = both.astype(jnp.bfloat16)


def prepare_kernel(hidden, weight, passages, cands, counts, permitted, packed, own):
    pack_kernel(hidden, weight, packed)
    stock_kernel(passages, cands, counts, permitted, own)


def prepare(hidden, weight, passages, cands, counts, permitted):
    return pl.pallas_call(
        prepare_kernel,
        out_shape=(
            jax.ShapeDtypeStruct((LANES, FOLD_ROWS + HID_DEV, 128), jnp.bfloat16),
            jax.ShapeDtypeStruct((ROWS, DIM), jnp.bfloat16),
        ),
        in_specs=[vmem()] * 6,
        out_specs=(vmem(), vmem()),
        compiler_params=limit(56),
        name="prepare",
    )(hidden, weight, passages, cands, counts, permitted)


def both_kernel(own, across, out):
    out[0:ROWS, :] = own[...]
    out[ROWS : 2 * ROWS, :] = across[...]


def both(own, across):
    return pl.pallas_call(
        both_kernel,
        out_shape=jax.ShapeDtypeStruct((2 * ROWS, DIM), jnp.bfloat16),
        in_specs=[vmem()] * 2,
        out_specs=vmem(),
        cost_estimate=pl.CostEstimate(
            flops=40 * 10**9, bytes_accessed=4 * ROWS * DIM * 2, transcendentals=0
        ),
        compiler_params=limit(8),
        name="both",
    )(own, across)


def all_four_kernel(*refs):
    for i, ref in enumerate(refs[:4]):
        refs[4][2 * ROWS * i : 2 * ROWS * (i + 1), :] = ref[...]


def all_four(*pairs):
    return pl.pallas_call(
        all_four_kernel,
        out_shape=jax.ShapeDtypeStruct((8 * ROWS, DIM), jnp.bfloat16),
        in_specs=[vmem()] * 4,
        out_specs=vmem(),
        cost_estimate=pl.CostEstimate(
            flops=10 * 10**9, bytes_accessed=16 * ROWS * DIM * 2, transcendentals=0
        ),
        compiler_params=limit(14),
        name="all_four",
    )(*pairs)


def project_kernel(packed, out):
    hidden_rows = []
    weight_rows = [[] for _ in range(FOLD)]
    for source in range(LANES):
        block = packed[source].astype(jnp.float32)
        hidden_rows.append(block[0:FOLD_ROWS])
        for c in range(FOLD):
            start = FOLD_ROWS * (1 + c)
            weight_rows[c].append(block[start : start + FOLD_ROWS])
    hidden = jnp.concatenate(hidden_rows, axis=0).astype(jnp.bfloat16)
    projected = jnp.zeros((QT, DIM), jnp.float32)
    for c in range(FOLD):
        weight = jnp.concatenate(weight_rows[c], axis=0).astype(jnp.bfloat16)
        product = lax.dot_general(
            hidden, weight, (((0,), (0,)), ((), ())), preferred_element_type=jnp.float32
        )
        projected = projected + product[QT * c : QT * (c + 1), :]
    squares = jnp.sum(projected * projected, axis=1, keepdims=True)
    rows = (projected * lax.rsqrt(squares + 1e-06)).astype(jnp.bfloat16)
    for lane in range(LANES):
        out[lane] = rows


def project(packed):
    return pl.pallas_call(
        project_kernel,
        out_shape=jax.ShapeDtypeStruct((LANES, QT, DIM), jnp.bfloat16),
        in_specs=[vmem()],
        out_specs=vmem(),
        cost_estimate=pl.CostEstimate(
            flops=20 * 10**9, bytes_accessed=LANES * QT * DIM * 2, transcendentals=0
        ),
        compiler_params=limit(8),
        name="project",
    )(packed)


def three_parts(value):
    first = value.astype(jnp.bfloat16)
    rest = value - first.astype(jnp.float32)
    second = rest.astype(jnp.bfloat16)
    third = (rest - second.astype(jnp.float32)).astype(jnp.bfloat16)
    return first, second, third


def turn_kernel(queries, out):
    out[...] = queries[...].astype(jnp.float32).T.astype(jnp.bfloat16)


def turn(queries):
    return pl.pallas_call(
        turn_kernel,
        out_shape=jax.ShapeDtypeStruct((DIM, TOK), jnp.bfloat16),
        in_specs=[vmem()],
        out_specs=vmem(),
        cost_estimate=pl.CostEstimate(
            flops=40 * 10**9, bytes_accessed=2 * TOK * DIM * 2, transcendentals=0
        ),
        compiler_params=limit(8),
        name="turn",
    )(queries)


def score_kernel(group, turned, *refs):
    blocks, (out, best, masks) = refs[:SIDES], refs[SIDES:]
    step = pl.program_id(0)

    quarter = group[0] // FOLD
    for side, block in enumerate(blocks):
        for c in range(TOK // 256):
            part = turned[:, 256 * c : 256 * (c + 1)]
            similarity = jnp.dot(
                block[0:STOCK_ROWS, :], part, preferred_element_type=jnp.float32
            )
            top = jnp.max(similarity.reshape(P_DEV, PT, 256), axis=1)
            best[side, step, :, 256 * c : 256 * (c + 1)] = top
        mask = block[STOCK_ROWS:ROWS, :].astype(jnp.float32)
        picked = mask[0:P_DEV]
        for b in range(1, QUERIES // 128):
            picked = jnp.where(quarter == b, mask[P_DEV * b : P_DEV * (b + 1)], picked)
        masks[side, step] = picked

    @pl.when(step == STEPS - 1)
    def _():
        tops = best[...].reshape(GROUPS * P_DEV, TOK)
        member = (row_index((QT, TOK)) == lane_index((QT, TOK)) // QT).astype(jnp.bfloat16)
        scores = jnp.zeros((QT, GROUPS * P_DEV), jnp.float32)
        for part in three_parts(tops):
            scores = scores + lax.dot_general(
                member, part, (((1,), (1,)), ((), ())), preferred_element_type=jnp.float32
            )
        lane = lax.rem(row_index((LANES, 128)) + FIRST, LANES)
        wanted = (group[0] % FOLD) * LANES + lane
        chosen = (lane_index((QT, 128)) == wanted).astype(jnp.bfloat16)
        live = lax.dot_general(
            chosen,
            masks[...].reshape(GROUPS * P_DEV, 128).astype(jnp.bfloat16),
            (((1,), (1,)), ((), ())),
            preferred_element_type=jnp.float32,
        )
        out[...] = jnp.where(live > 0.5, scores, 0.0)


def score(group, queries, mine, theirs):
    return pl.pallas_call(
        score_kernel,
        out_shape=jax.ShapeDtypeStruct((QT, GROUPS * P_DEV), jnp.float32),
        grid=(STEPS,),
        in_specs=[
            pl.BlockSpec(memory_space=pltpu.SMEM),
            pl.BlockSpec((DIM, TOK), lambda i: (0, 0)),
            *[
                pl.BlockSpec((ROWS, DIM), lambda i, at=at: (i + at * STEPS, 0))
                for at in range(SIDES // 2)
            ]
            * 2,
        ],
        out_specs=pl.BlockSpec((QT, GROUPS * P_DEV), lambda i: (0, 0)),
        scratch_shapes=[
            pltpu.VMEM((SIDES, STEPS, P_DEV, TOK), jnp.float32),
            pltpu.VMEM((SIDES, STEPS, P_DEV, 128), jnp.float32),
        ],
        cost_estimate=pl.CostEstimate(
            flops=40 * 10**9, bytes_accessed=GROUPS * ROWS * DIM * 2, transcendentals=0
        ),
        compiler_params=limit(16),
        name="score",
    )(group, queries, *[mine] * (SIDES // 2), *[theirs] * (SIDES // 2))


def split_exchange(arrays, distance):
    count = len(arrays)
    if distance < count:
        result = list(arrays)
        for i in range(count):
            if not i & distance:
                result[i] = jnp.maximum(arrays[i], arrays[i + distance])
                result[i + distance] = jnp.minimum(arrays[i], arrays[i + distance])
        return result
    rows = distance // count
    upper = (row_index((8, 128)) & rows) != 0
    result = []
    for array in arrays:
        down = pltpu.roll(array, rows, 0)
        partner = down if 2 * rows == 8 else jnp.where(upper, down, pltpu.roll(array, 8 - rows, 0))
        result.append(jnp.where(upper, jnp.minimum(array, partner), jnp.maximum(array, partner)))
    return result


def select_kernel(table, out):
    arrays = []
    for v in range(LANES // 8):
        base = table[8 * v : 8 * (v + 1), :]
        arrays.append(base)
        for k in range(1, FOLD):
            arrays.append(pltpu.roll(base, QT * k, 1))
    arrays = [jnp.maximum(array, 0.0) for array in arrays]
    count = len(arrays)
    rows = row_index((8, 128))
    lanes = lane_index((8, 128))

    def signs(bit):
        return jnp.where((lanes & bit) != 0, -1.0, 1.0)

    column_sign = signs(16)
    arrays = [array * column_sign for array in arrays]
    size = 2
    while size <= K:
        flips = []
        for i in range(count):
            if size < count:
                flips.append(-1.0 if i & size else 1.0)
            elif size < K:
                flips.append(jnp.where((rows & (size // count)) != 0, -1.0, 1.0))
            else:
                flips.append(1.0)

        def flipped(values):
            return [v if isinstance(f, float) and f == 1.0 else v * f for v, f in zip(values, flips)]

        arrays = flipped(arrays)
        distance = size // 2
        while distance:
            arrays = split_exchange(arrays, distance)
            distance //= 2
        arrays = flipped(arrays)
        size *= 2
    width = 16
    while width:
        arrays = [array * column_sign for array in arrays]
        arrays = [jnp.maximum(array, pltpu.roll(array, width, 1)) for array in arrays]
        width //= 2
        if width:
            column_sign = signs(width)
            arrays = [array * column_sign for array in arrays]
        distance = K // 2
        while distance:
            arrays = split_exchange(arrays, distance)
            distance //= 2
    total = jnp.zeros((8, 128), jnp.float32)
    for i, array in enumerate(arrays):
        total = total + jnp.where(lanes == rows * count + i, array, 0.0)
    out[...] = jnp.sum(total, axis=0, keepdims=True)


def select(table):
    return pl.pallas_call(
        select_kernel,
        out_shape=jax.ShapeDtypeStruct((1, K), jnp.float32),
        in_specs=[vmem()],
        out_specs=vmem(),
        compiler_params=limit(8),
        name="select",
    )(table)


def exchanged(blocks):
    order = [(FIRST + k) % LANES for k in range(LANES)]
    return lax.all_to_all(blocks, "shard", 0, 0, tiled=True, axis_index_groups=[order])


def turned(steps):
    return [(i, (i + steps) % GROUPS) for i in range(GROUPS)]


def body(hidden, proj_weight, passages, cands, counts, permitted):
    group = lax.axis_index("blk").astype(jnp.int32).reshape(1)
    slots = cands.reshape(QUERIES, CAND).T
    packed, own = prepare(
        hidden,
        proj_weight,
        passages.reshape(STOCK_ROWS, DIM),
        slots,
        counts.reshape(1, QUERIES),
        permitted,
    )
    across = lax.ppermute(own, "blk", [(i, i ^ 2) for i in range(GROUPS)])
    pair = both(own, across)
    along_x = [lax.ppermute(pair, "blk", turned(4 * x)) for x in (1, 3, 2)]
    rows = project(exchanged(packed))
    mine = all_four(pair, *along_x)
    theirs = lax.ppermute(mine, "blk", [(i, i ^ 1) for i in range(GROUPS)])
    queries = exchanged(rows).reshape(TOK, DIM)
    table = score(group, turn(queries), mine, theirs)
    entries = exchanged(table.reshape(LANES, 1, 128))
    return select(entries.reshape(LANES, 128))


def solution(mesh):
    in_specs = (
        P("shard", "blk"),
        P("shard", None),
        P(("blk", "shard"), None, None),
        P("blk", "shard", None, None),
        P("blk", "shard", None),
        P("blk", None),
    )
    out_specs = P(("blk", "shard"), None)
    return jax.shard_map(body, mesh=mesh, in_specs=in_specs, out_specs=out_specs, check_vma=False)
```

```python
import jax
import jax.numpy as jnp
from jax import lax
from jax.experimental import pallas as pl
from jax.experimental.pallas import tpu as pltpu
from jax.sharding import PartitionSpec as P

DIM = 128
HID = 1024
QT = 32
PT = 128
CAND = 4
K = 128
P_DEV = 8
GROUPS = 16
LANES = 32
QUERIES = 512
TOK = QUERIES // GROUPS * QT
HID_DEV = HID // LANES
STOCK_ROWS = P_DEV * PT
MASK_ROWS = P_DEV * QUERIES // 128
ROWS = STOCK_ROWS + MASK_ROWS
STEPS = 2
SIDES = GROUPS // STEPS
FOLD = 128 // QT
FOLD_ROWS = HID_DEV // FOLD
FIRST = 8
FIRST_PACKED = 10


def vmem():
    return pl.BlockSpec(memory_space=pltpu.VMEM)


def limit(mebibytes):
    return pltpu.CompilerParams(vmem_limit_bytes=mebibytes * 2**20)


def lane_index(shape):
    return lax.broadcasted_iota(jnp.int32, shape, 1)


def row_index(shape):
    return lax.broadcasted_iota(jnp.int32, shape, 0)


def stock_kernel(passages, cands, counts, permitted, out):
    out[0:STOCK_ROWS, :] = passages[...]
    slots = row_index((P_DEV, QUERIES))
    allowed = permitted[...] == 1
    counted = counts[...]
    live = jnp.zeros((P_DEV, QUERIES), jnp.float32)
    for j in range(CAND):
        use = jnp.where(allowed & (counted > j), cands[j : j + 1, :], -1)
        live = jnp.where(use == slots, 1.0, live)
    parts = [live[:, 128 * b : 128 * (b + 1)] for b in range(QUERIES // 128)]
    out[STOCK_ROWS:ROWS, :] = jnp.concatenate(parts, axis=0).astype(jnp.bfloat16)


def pack_kernel(hidden, weight, out):
    weight_rows = weight[...].astype(jnp.float32)
    slot = lane_index((FOLD_ROWS, 128)) // QT
    for tile in range(TOK // 128):
        block = hidden[:, 128 * tile : 128 * (tile + 1)].astype(jnp.float32)
        bands = [block[FOLD_ROWS * c : FOLD_ROWS * (c + 1), :] for c in range(FOLD)]
        for k in range(FOLD):
            folded = bands[k]
            for c in range(FOLD):
                if c != k:
                    moved = pltpu.roll(bands[c], (QT * (c - k)) % 128, 1)
                    folded = jnp.where(slot == c, moved, folded)
            both = jnp.concatenate([folded, weight_rows], axis=0)
            out[(tile * FOLD + k - FIRST_PACKED) % LANES] = both.astype(jnp.bfloat16)


def prepare_kernel(hidden, weight, passages, cands, counts, permitted, packed, own):
    pack_kernel(hidden, weight, packed)
    stock_kernel(passages, cands, counts, permitted, own)


def prepare(hidden, weight, passages, cands, counts, permitted):
    return pl.pallas_call(
        prepare_kernel,
        out_shape=(
            jax.ShapeDtypeStruct((LANES, FOLD_ROWS + HID_DEV, 128), jnp.bfloat16),
            jax.ShapeDtypeStruct((ROWS, DIM), jnp.bfloat16),
        ),
        in_specs=[vmem()] * 6,
        out_specs=(vmem(), vmem()),
        compiler_params=limit(56),
        name="prepare",
    )(hidden, weight, passages, cands, counts, permitted)


def both_kernel(own, across, out):
    out[0:ROWS, :] = own[...]
    out[ROWS : 2 * ROWS, :] = across[...]


def both(own, across):
    return pl.pallas_call(
        both_kernel,
        out_shape=jax.ShapeDtypeStruct((2 * ROWS, DIM), jnp.bfloat16),
        in_specs=[vmem()] * 2,
        out_specs=vmem(),
        cost_estimate=pl.CostEstimate(
            flops=40 * 10**9, bytes_accessed=4 * ROWS * DIM * 2, transcendentals=0
        ),
        compiler_params=limit(8),
        name="both",
    )(own, across)


def all_four_kernel(*refs):
    for i, ref in enumerate(refs[:4]):
        refs[4][2 * ROWS * i : 2 * ROWS * (i + 1), :] = ref[...]


def all_four(*pairs):
    return pl.pallas_call(
        all_four_kernel,
        out_shape=jax.ShapeDtypeStruct((8 * ROWS, DIM), jnp.bfloat16),
        in_specs=[vmem()] * 4,
        out_specs=vmem(),
        cost_estimate=pl.CostEstimate(
            flops=10 * 10**9, bytes_accessed=16 * ROWS * DIM * 2, transcendentals=0
        ),
        compiler_params=limit(14),
        name="all_four",
    )(*pairs)


def project_kernel(packed, out):
    hidden_rows = []
    weight_rows = [[] for _ in range(FOLD)]
    for source in range(LANES):
        block = packed[source].astype(jnp.float32)
        hidden_rows.append(block[0:FOLD_ROWS])
        for c in range(FOLD):
            start = FOLD_ROWS * (1 + c)
            weight_rows[c].append(block[start : start + FOLD_ROWS])
    hidden = jnp.concatenate(hidden_rows, axis=0).astype(jnp.bfloat16)
    projected = jnp.zeros((QT, DIM), jnp.float32)
    for c in range(FOLD):
        weight = jnp.concatenate(weight_rows[c], axis=0).astype(jnp.bfloat16)
        product = lax.dot_general(
            hidden, weight, (((0,), (0,)), ((), ())), preferred_element_type=jnp.float32
        )
        projected = projected + product[QT * c : QT * (c + 1), :]
    squares = jnp.sum(projected * projected, axis=1, keepdims=True)
    rows = (projected * lax.rsqrt(squares + 1e-06)).astype(jnp.bfloat16)
    for lane in range(LANES):
        out[lane] = rows


def project(packed):
    return pl.pallas_call(
        project_kernel,
        out_shape=jax.ShapeDtypeStruct((LANES, QT, DIM), jnp.bfloat16),
        in_specs=[vmem()],
        out_specs=vmem(),
        cost_estimate=pl.CostEstimate(
            flops=20 * 10**9, bytes_accessed=LANES * QT * DIM * 2, transcendentals=0
        ),
        compiler_params=limit(8),
        name="project",
    )(packed)


def three_parts(value):
    first = value.astype(jnp.bfloat16)
    rest = value - first.astype(jnp.float32)
    second = rest.astype(jnp.bfloat16)
    third = (rest - second.astype(jnp.float32)).astype(jnp.bfloat16)
    return first, second, third


def turn_kernel(queries, out):
    out[...] = queries[...].astype(jnp.float32).T.astype(jnp.bfloat16)


def turn(queries):
    return pl.pallas_call(
        turn_kernel,
        out_shape=jax.ShapeDtypeStruct((DIM, TOK), jnp.bfloat16),
        in_specs=[vmem()],
        out_specs=vmem(),
        cost_estimate=pl.CostEstimate(
            flops=40 * 10**9, bytes_accessed=2 * TOK * DIM * 2, transcendentals=0
        ),
        compiler_params=limit(8),
        name="turn",
    )(queries)


def score_kernel(group, turned, *refs):
    blocks, (out, best, masks) = refs[:SIDES], refs[SIDES:]
    step = pl.program_id(0)

    quarter = group[0] // FOLD
    for side, block in enumerate(blocks):
        for c in range(TOK // 256):
            part = turned[:, 256 * c : 256 * (c + 1)]
            similarity = jnp.dot(
                block[0:STOCK_ROWS, :], part, preferred_element_type=jnp.float32
            )
            top = jnp.max(similarity.reshape(P_DEV, PT, 256), axis=1)
            best[side, step, :, 256 * c : 256 * (c + 1)] = top
        mask = block[STOCK_ROWS:ROWS, :].astype(jnp.float32)
        picked = mask[0:P_DEV]
        for b in range(1, QUERIES // 128):
            picked = jnp.where(quarter == b, mask[P_DEV * b : P_DEV * (b + 1)], picked)
        masks[side, step] = picked

    @pl.when(step == STEPS - 1)
    def _():
        tops = best[...].reshape(GROUPS * P_DEV, TOK)
        member = (row_index((QT, TOK)) == lane_index((QT, TOK)) // QT).astype(jnp.bfloat16)
        scores = jnp.zeros((QT, GROUPS * P_DEV), jnp.float32)
        for part in three_parts(tops):
            scores = scores + lax.dot_general(
                member, part, (((1,), (1,)), ((), ())), preferred_element_type=jnp.float32
            )
        lane = lax.rem(row_index((LANES, 128)) + FIRST, LANES)
        wanted = (group[0] % FOLD) * LANES + lane
        chosen = (lane_index((QT, 128)) == wanted).astype(jnp.bfloat16)
        live = lax.dot_general(
            chosen,
            masks[...].reshape(GROUPS * P_DEV, 128).astype(jnp.bfloat16),
            (((1,), (1,)), ((), ())),
            preferred_element_type=jnp.float32,
        )
        out[...] = jnp.where(live > 0.5, scores, 0.0)


def score(group, queries, mine, theirs):
    return pl.pallas_call(
        score_kernel,
        out_shape=jax.ShapeDtypeStruct((QT, GROUPS * P_DEV), jnp.float32),
        grid=(STEPS,),
        in_specs=[
            pl.BlockSpec(memory_space=pltpu.SMEM),
            pl.BlockSpec((DIM, TOK), lambda i: (0, 0)),
            *[
                pl.BlockSpec((ROWS, DIM), lambda i, at=at: (i + at * STEPS, 0))
                for at in range(SIDES // 2)
            ]
            * 2,
        ],
        out_specs=pl.BlockSpec((QT, GROUPS * P_DEV), lambda i: (0, 0)),
        scratch_shapes=[
            pltpu.VMEM((SIDES, STEPS, P_DEV, TOK), jnp.float32),
            pltpu.VMEM((SIDES, STEPS, P_DEV, 128), jnp.float32),
        ],
        cost_estimate=pl.CostEstimate(
            flops=40 * 10**9, bytes_accessed=GROUPS * ROWS * DIM * 2, transcendentals=0
        ),
        compiler_params=limit(16),
        name="score",
    )(group, queries, *[mine] * (SIDES // 2), *[theirs] * (SIDES // 2))


def split_exchange(arrays, distance):
    count = len(arrays)
    if distance < count:
        result = list(arrays)
        for i in range(count):
            if not i & distance:
                result[i] = jnp.maximum(arrays[i], arrays[i + distance])
                result[i + distance] = jnp.minimum(arrays[i], arrays[i + distance])
        return result
    rows = distance // count
    upper = (row_index((8, 128)) & rows) != 0
    result = []
    for array in arrays:
        down = pltpu.roll(array, rows, 0)
        partner = down if 2 * rows == 8 else jnp.where(upper, down, pltpu.roll(array, 8 - rows, 0))
        result.append(jnp.where(upper, jnp.minimum(array, partner), jnp.maximum(array, partner)))
    return result


def select_kernel(table, out):
    arrays = []
    for v in range(LANES // 8):
        base = table[8 * v : 8 * (v + 1), :]
        arrays.append(base)
        for k in range(1, FOLD):
            arrays.append(pltpu.roll(base, QT * k, 1))
    arrays = [jnp.maximum(array, 0.0) for array in arrays]
    count = len(arrays)
    rows = row_index((8, 128))
    lanes = lane_index((8, 128))

    def signs(bit):
        return jnp.where((lanes & bit) != 0, -1.0, 1.0)

    column_sign = signs(16)
    arrays = [array * column_sign for array in arrays]
    size = 2
    while size <= K:
        flips = []
        for i in range(count):
            if size < count:
                flips.append(-1.0 if i & size else 1.0)
            elif size < K:
                flips.append(jnp.where((rows & (size // count)) != 0, -1.0, 1.0))
            else:
                flips.append(1.0)

        def flipped(values):
            return [v if isinstance(f, float) and f == 1.0 else v * f for v, f in zip(values, flips)]

        arrays = flipped(arrays)
        distance = size // 2
        while distance:
            arrays = split_exchange(arrays, distance)
            distance //= 2
        arrays = flipped(arrays)
        size *= 2
    width = 16
    while width:
        arrays = [array * column_sign for array in arrays]
        arrays = [jnp.maximum(array, pltpu.roll(array, width, 1)) for array in arrays]
        width //= 2
        if width:
            column_sign = signs(width)
            arrays = [array * column_sign for array in arrays]
        distance = K // 2
        while distance:
            arrays = split_exchange(arrays, distance)
            distance //= 2
    total = jnp.zeros((8, 128), jnp.float32)
    for i, array in enumerate(arrays):
        total = total + jnp.where(lanes == rows * count + i, array, 0.0)
    out[...] = jnp.sum(total, axis=0, keepdims=True)


def select(table):
    return pl.pallas_call(
        select_kernel,
        out_shape=jax.ShapeDtypeStruct((1, K), jnp.float32),
        in_specs=[vmem()],
        out_specs=vmem(),
        compiler_params=limit(8),
        name="select",
    )(table)


def exchanged(blocks, first=FIRST):
    order = [(first + k) % LANES for k in range(LANES)]
    return lax.all_to_all(blocks, "shard", 0, 0, tiled=True, axis_index_groups=[order])


def turned(steps):
    return [(i, (i + steps) % GROUPS) for i in range(GROUPS)]


def body(hidden, proj_weight, passages, cands, counts, permitted):
    group = lax.axis_index("blk").astype(jnp.int32).reshape(1)
    slots = cands.reshape(QUERIES, CAND).T
    packed, own = prepare(
        hidden,
        proj_weight,
        passages.reshape(STOCK_ROWS, DIM),
        slots,
        counts.reshape(1, QUERIES),
        permitted,
    )
    across = lax.ppermute(own, "blk", [(i, i ^ 2) for i in range(GROUPS)])
    pair = both(own, across)
    along_x = [lax.ppermute(pair, "blk", turned(4 * x)) for x in (1, 3, 2)]
    rows = project(exchanged(packed, FIRST_PACKED))
    mine = all_four(pair, *along_x)
    theirs = lax.ppermute(mine, "blk", [(i, i ^ 1) for i in range(GROUPS)])
    queries = exchanged(rows).reshape(TOK, DIM)
    table = score(group, turn(queries), mine, theirs)
    entries = exchanged(table.reshape(LANES, 1, 128))
    return select(entries.reshape(LANES, 128))


def solution(mesh):
    in_specs = (
        P("shard", "blk"),
        P("shard", None),
        P(("blk", "shard"), None, None),
        P("blk", "shard", None, None),
        P("blk", "shard", None),
        P("blk", None),
    )
    out_specs = P(("blk", "shard"), None)
    return jax.shard_map(body, mesh=mesh, in_specs=in_specs, out_specs=out_specs, check_vma=False)
```

```python
import jax
import jax.numpy as jnp
from jax import lax
from jax.experimental import pallas as pl
from jax.experimental.pallas import tpu as pltpu
from jax.sharding import PartitionSpec as P

DIM = 128
HID = 1024
QT = 32
PT = 128
CAND = 4
K = 128
P_DEV = 8
GROUPS = 16
LANES = 32
QUERIES = 512
TOK = QUERIES // GROUPS * QT
HID_DEV = HID // LANES
STOCK_ROWS = P_DEV * PT
MASK_ROWS = P_DEV * QUERIES // 128
ROWS = STOCK_ROWS + MASK_ROWS
STEPS = 2
SIDES = GROUPS // STEPS
FOLD = 128 // QT
FOLD_ROWS = HID_DEV // FOLD
FIRST = 10


def vmem():
    return pl.BlockSpec(memory_space=pltpu.VMEM)


def limit(mebibytes):
    return pltpu.CompilerParams(vmem_limit_bytes=mebibytes * 2**20)


def lane_index(shape):
    return lax.broadcasted_iota(jnp.int32, shape, 1)


def row_index(shape):
    return lax.broadcasted_iota(jnp.int32, shape, 0)


def stock_kernel(passages, cands, counts, permitted, out):
    out[0:STOCK_ROWS, :] = passages[...]
    slots = row_index((P_DEV, QUERIES))
    allowed = permitted[...] == 1
    counted = counts[...]
    live = jnp.zeros((P_DEV, QUERIES), jnp.float32)
    for j in range(CAND):
        use = jnp.where(allowed & (counted > j), cands[j : j + 1, :], -1)
        live = jnp.where(use == slots, 1.0, live)
    parts = [live[:, 128 * b : 128 * (b + 1)] for b in range(QUERIES // 128)]
    out[STOCK_ROWS:ROWS, :] = jnp.concatenate(parts, axis=0).astype(jnp.bfloat16)


def pack_kernel(hidden, weight, out):
    weight_rows = weight[...].astype(jnp.float32)
    slot = lane_index((FOLD_ROWS, 128)) // QT
    for tile in range(TOK // 128):
        block = hidden[:, 128 * tile : 128 * (tile + 1)].astype(jnp.float32)
        bands = [block[FOLD_ROWS * c : FOLD_ROWS * (c + 1), :] for c in range(FOLD)]
        for k in range(FOLD):
            folded = bands[k]
            for c in range(FOLD):
                if c != k:
                    moved = pltpu.roll(bands[c], (QT * (c - k)) % 128, 1)
                    folded = jnp.where(slot == c, moved, folded)
            both = jnp.concatenate([folded, weight_rows], axis=0)
            out[(tile * FOLD + k - FIRST) % LANES] = both.astype(jnp.bfloat16)


def prepare_kernel(hidden, weight, passages, cands, counts, permitted, packed, own):
    pack_kernel(hidden, weight, packed)
    stock_kernel(passages, cands, counts, permitted, own)


def prepare(hidden, weight, passages, cands, counts, permitted):
    return pl.pallas_call(
        prepare_kernel,
        out_shape=(
            jax.ShapeDtypeStruct((LANES, FOLD_ROWS + HID_DEV, 128), jnp.bfloat16),
            jax.ShapeDtypeStruct((ROWS, DIM), jnp.bfloat16),
        ),
        in_specs=[vmem()] * 6,
        out_specs=(vmem(), vmem()),
        compiler_params=limit(56),
        name="prepare",
    )(hidden, weight, passages, cands, counts, permitted)


def both_kernel(own, across, out):
    out[0:ROWS, :] = own[...]
    out[ROWS : 2 * ROWS, :] = across[...]


def both(own, across):
    return pl.pallas_call(
        both_kernel,
        out_shape=jax.ShapeDtypeStruct((2 * ROWS, DIM), jnp.bfloat16),
        in_specs=[vmem()] * 2,
        out_specs=vmem(),
        cost_estimate=pl.CostEstimate(
            flops=40 * 10**9, bytes_accessed=4 * ROWS * DIM * 2, transcendentals=0
        ),
        compiler_params=limit(8),
        name="both",
    )(own, across)


def all_four_kernel(*refs):
    for i, ref in enumerate(refs[:4]):
        refs[4][2 * ROWS * i : 2 * ROWS * (i + 1), :] = ref[...]


def all_four(*pairs):
    return pl.pallas_call(
        all_four_kernel,
        out_shape=jax.ShapeDtypeStruct((8 * ROWS, DIM), jnp.bfloat16),
        in_specs=[vmem()] * 4,
        out_specs=vmem(),
        cost_estimate=pl.CostEstimate(
            flops=10 * 10**9, bytes_accessed=16 * ROWS * DIM * 2, transcendentals=0
        ),
        compiler_params=limit(14),
        name="all_four",
    )(*pairs)


def project_kernel(packed, out):
    hidden_rows = []
    weight_rows = [[] for _ in range(FOLD)]
    for source in range(LANES):
        block = packed[source].astype(jnp.float32)
        hidden_rows.append(block[0:FOLD_ROWS])
        for c in range(FOLD):
            start = FOLD_ROWS * (1 + c)
            weight_rows[c].append(block[start : start + FOLD_ROWS])
    hidden = jnp.concatenate(hidden_rows, axis=0).astype(jnp.bfloat16)
    projected = jnp.zeros((QT, DIM), jnp.float32)
    for c in range(FOLD):
        weight = jnp.concatenate(weight_rows[c], axis=0).astype(jnp.bfloat16)
        product = lax.dot_general(
            hidden, weight, (((0,), (0,)), ((), ())), preferred_element_type=jnp.float32
        )
        projected = projected + product[QT * c : QT * (c + 1), :]
    squares = jnp.sum(projected * projected, axis=1, keepdims=True)
    rows = (projected * lax.rsqrt(squares + 1e-06)).astype(jnp.bfloat16)
    for lane in range(LANES):
        out[lane] = rows


def project(packed):
    return pl.pallas_call(
        project_kernel,
        out_shape=jax.ShapeDtypeStruct((LANES, QT, DIM), jnp.bfloat16),
        in_specs=[vmem()],
        out_specs=vmem(),
        cost_estimate=pl.CostEstimate(
            flops=20 * 10**9, bytes_accessed=LANES * QT * DIM * 2, transcendentals=0
        ),
        compiler_params=limit(8),
        name="project",
    )(packed)


def three_parts(value):
    first = value.astype(jnp.bfloat16)
    rest = value - first.astype(jnp.float32)
    second = rest.astype(jnp.bfloat16)
    third = (rest - second.astype(jnp.float32)).astype(jnp.bfloat16)
    return first, second, third


def turn_kernel(queries, out):
    out[...] = queries[...].astype(jnp.float32).T.astype(jnp.bfloat16)


def turn(queries):
    return pl.pallas_call(
        turn_kernel,
        out_shape=jax.ShapeDtypeStruct((DIM, TOK), jnp.bfloat16),
        in_specs=[vmem()],
        out_specs=vmem(),
        cost_estimate=pl.CostEstimate(
            flops=40 * 10**9, bytes_accessed=2 * TOK * DIM * 2, transcendentals=0
        ),
        compiler_params=limit(8),
        name="turn",
    )(queries)


def score_kernel(group, turned, *refs):
    blocks, (out, best, masks) = refs[:SIDES], refs[SIDES:]
    step = pl.program_id(0)

    quarter = group[0] // FOLD
    for side, block in enumerate(blocks):
        for c in range(TOK // 256):
            part = turned[:, 256 * c : 256 * (c + 1)]
            similarity = jnp.dot(
                block[0:STOCK_ROWS, :], part, preferred_element_type=jnp.float32
            )
            top = jnp.max(similarity.reshape(P_DEV, PT, 256), axis=1)
            best[side, step, :, 256 * c : 256 * (c + 1)] = top
        mask = block[STOCK_ROWS:ROWS, :].astype(jnp.float32)
        picked = mask[0:P_DEV]
        for b in range(1, QUERIES // 128):
            picked = jnp.where(quarter == b, mask[P_DEV * b : P_DEV * (b + 1)], picked)
        masks[side, step] = picked

    @pl.when(step == STEPS - 1)
    def _():
        tops = best[...].reshape(GROUPS * P_DEV, TOK)
        member = (row_index((QT, TOK)) == lane_index((QT, TOK)) // QT).astype(jnp.bfloat16)
        scores = jnp.zeros((QT, GROUPS * P_DEV), jnp.float32)
        for part in three_parts(tops):
            scores = scores + lax.dot_general(
                member, part, (((1,), (1,)), ((), ())), preferred_element_type=jnp.float32
            )
        lane = lax.rem(row_index((LANES, 128)) + FIRST, LANES)
        wanted = (group[0] % FOLD) * LANES + lane
        chosen = (lane_index((QT, 128)) == wanted).astype(jnp.bfloat16)
        live = lax.dot_general(
            chosen,
            masks[...].reshape(GROUPS * P_DEV, 128).astype(jnp.bfloat16),
            (((1,), (1,)), ((), ())),
            preferred_element_type=jnp.float32,
        )
        out[...] = jnp.where(live > 0.5, scores, 0.0)


def score(group, queries, mine, theirs):
    return pl.pallas_call(
        score_kernel,
        out_shape=jax.ShapeDtypeStruct((QT, GROUPS * P_DEV), jnp.float32),
        grid=(STEPS,),
        in_specs=[
            pl.BlockSpec(memory_space=pltpu.SMEM),
            pl.BlockSpec((DIM, TOK), lambda i: (0, 0)),
            *[
                pl.BlockSpec((ROWS, DIM), lambda i, at=at: (i + at * STEPS, 0))
                for at in range(SIDES // 2)
            ]
            * 2,
        ],
        out_specs=pl.BlockSpec((QT, GROUPS * P_DEV), lambda i: (0, 0)),
        scratch_shapes=[
            pltpu.VMEM((SIDES, STEPS, P_DEV, TOK), jnp.float32),
            pltpu.VMEM((SIDES, STEPS, P_DEV, 128), jnp.float32),
        ],
        cost_estimate=pl.CostEstimate(
            flops=40 * 10**9, bytes_accessed=GROUPS * ROWS * DIM * 2, transcendentals=0
        ),
        compiler_params=limit(16),
        name="score",
    )(group, queries, *[mine] * (SIDES // 2), *[theirs] * (SIDES // 2))


def split_exchange(arrays, distance):
    count = len(arrays)
    if distance < count:
        result = list(arrays)
        for i in range(count):
            if not i & distance:
                result[i] = jnp.maximum(arrays[i], arrays[i + distance])
                result[i + distance] = jnp.minimum(arrays[i], arrays[i + distance])
        return result
    rows = distance // count
    upper = (row_index((8, 128)) & rows) != 0
    result = []
    for array in arrays:
        down = pltpu.roll(array, rows, 0)
        partner = down if 2 * rows == 8 else jnp.where(upper, down, pltpu.roll(array, 8 - rows, 0))
        result.append(jnp.where(upper, jnp.minimum(array, partner), jnp.maximum(array, partner)))
    return result


def select_kernel(table, out):
    arrays = []
    for v in range(LANES // 8):
        base = table[8 * v : 8 * (v + 1), :]
        arrays.append(base)
        for k in range(1, FOLD):
            arrays.append(pltpu.roll(base, QT * k, 1))
    arrays = [jnp.maximum(array, 0.0) for array in arrays]
    count = len(arrays)
    rows = row_index((8, 128))
    lanes = lane_index((8, 128))

    def signs(bit):
        return jnp.where((lanes & bit) != 0, -1.0, 1.0)

    column_sign = signs(16)
    arrays = [array * column_sign for array in arrays]
    size = 2
    while size <= K:
        flips = []
        for i in range(count):
            if size < count:
                flips.append(-1.0 if i & size else 1.0)
            elif size < K:
                flips.append(jnp.where((rows & (size // count)) != 0, -1.0, 1.0))
            else:
                flips.append(1.0)

        def flipped(values):
            return [v if isinstance(f, float) and f == 1.0 else v * f for v, f in zip(values, flips)]

        arrays = flipped(arrays)
        distance = size // 2
        while distance:
            arrays = split_exchange(arrays, distance)
            distance //= 2
        arrays = flipped(arrays)
        size *= 2
    width = 16
    while width:
        arrays = [array * column_sign for array in arrays]
        arrays = [jnp.maximum(array, pltpu.roll(array, width, 1)) for array in arrays]
        width //= 2
        if width:
            column_sign = signs(width)
            arrays = [array * column_sign for array in arrays]
        distance = K // 2
        while distance:
            arrays = split_exchange(arrays, distance)
            distance //= 2
    total = jnp.zeros((8, 128), jnp.float32)
    for i, array in enumerate(arrays):
        total = total + jnp.where(lanes == rows * count + i, array, 0.0)
    out[...] = jnp.sum(total, axis=0, keepdims=True)


def select(table):
    return pl.pallas_call(
        select_kernel,
        out_shape=jax.ShapeDtypeStruct((1, K), jnp.float32),
        in_specs=[vmem()],
        out_specs=vmem(),
        compiler_params=limit(8),
        name="select",
    )(table)


def exchanged(blocks):
    order = [(FIRST + k) % LANES for k in range(LANES)]
    return lax.all_to_all(blocks, "shard", 0, 0, tiled=True, axis_index_groups=[order])


def turned(steps):
    return [(i, (i + steps) % GROUPS) for i in range(GROUPS)]


def body(hidden, proj_weight, passages, cands, counts, permitted):
    group = lax.axis_index("blk").astype(jnp.int32).reshape(1)
    slots = cands.reshape(QUERIES, CAND).T
    packed, own = prepare(
        hidden,
        proj_weight,
        passages.reshape(STOCK_ROWS, DIM),
        slots,
        counts.reshape(1, QUERIES),
        permitted,
    )
    across = lax.ppermute(own, "blk", [(i, i ^ 2) for i in range(GROUPS)])
    pair = both(own, across)
    along_x = [lax.ppermute(pair, "blk", turned(4 * x)) for x in (1, 3, 2)]
    rows = project(exchanged(packed))
    mine = all_four(pair, *along_x)
    theirs = lax.ppermute(mine, "blk", [(i, i ^ 1) for i in range(GROUPS)])
    queries = exchanged(rows).reshape(TOK, DIM)
    table = score(group, turn(queries), mine, theirs)
    entries = exchanged(table.reshape(LANES, 1, 128))
    return select(entries.reshape(LANES, 128))


def solution(mesh):
    in_specs = (
        P("shard", "blk"),
        P("shard", None),
        P(("blk", "shard"), None, None),
        P("blk", "shard", None, None),
        P("blk", "shard", None),
        P("blk", None),
    )
    out_specs = P(("blk", "shard"), None)
    return jax.shard_map(body, mesh=mesh, in_specs=in_specs, out_specs=out_specs, check_vma=False)
```
